32 devices in a mesh: node: 4 (over y, x), batch: 8 (over z, core).
Axes of the slice: x: 2, y: 2, z: 4, core: 2. Of those that a mesh axis runs over, the one named last changes fastest.
Arguments:
- inputs: bfloat16 [8, 6, 64, 2048], P('batch', None, None, 'node'), may hold values from -6 to 6
- w_conv: bfloat16 [128, 128], replicated, may hold values from -0.5 to 0.5
- b_conv: float32 [128], replicated, may hold values from -3 to 3
- w_mix: bfloat16 [64, 320], replicated, may hold values from -0.3125 to 0.3125
- b_mix: float32 [64], replicated, may hold values from -3 to 3
- w_skip: bfloat16 [256, 64], replicated, may hold values from -0.75 to 0.75
- b_skip: float32 [256], replicated, may hold values from -3 to 3
- local_fwd: bfloat16 [2048, 384], P('node'), may hold values from -0.25 to 0.25
- local_bwd: bfloat16 [2048, 384], P('node'), may hold values from -0.25 to 0.25
- remote_fwd: bfloat16 [16, 128, 128], P('node'), may hold values from -0.25 to 0.25
- remote_bwd: bfloat16 [16, 128, 128], P('node'), may hold values from -0.25 to 0.25
- tile_src: int32 [16], P('node'), may hold values from 0 to 3, as said below
- tile_dst: int32 [16], P('node'), may hold values from -1 to 3, as said below
- residual_cotangent: bfloat16 [8, 4, 64, 2048], P('batch', None, None, 'node'), may hold values from -6 to 6
- cot_skip: bfloat16 [8, 256, 2048], P('batch', None, 'node'), may hold values from -6 to 6
Outputs:
- residual_out: bfloat16 [8, 4, 64, 2048], P('batch', None, None, 'node')
- skip_out: bfloat16 [8, 256, 2048], P('batch', None, 'node')
- grad_x: bfloat16 [8, 6, 64, 2048], P('batch', None, None, 'node')
- grad_w_conv: float32 [128, 128], replicated
- grad_b_conv: float32 [128], replicated
- grad_w_mix: float32 [64, 320], replicated
- grad_b_mix: float32 [64], replicated
- grad_w_skip: float32 [256, 64], replicated
- grad_b_skip: float32 [256], replicated
The draws below stay inside these ranges and needn't reach their ends.
Inputs may be any that keep to these rules, and one draw needn't show every extreme that they name: `tile_src`: entry p * 4 + q is a block of device p. `tile_dst`: entry p * 4 + q is a block of device q, or -1 where device p holds no tile for device q, always -1 for q = p.
All inputs are finite; a program needn't handle non-finite values.
Results may differ from the reference program's by a relative error of at most 0.012.
Values may be sent and summed in bfloat16 or wider, within the bound.
A program may use at most 128 MiB of HBM per device.

```python
import math
import jax
import jax.numpy as jnp
from jax import lax

HIDDEN_CHANNELS = 64
SKIP = 256
BLOCK = 128
T_IN = 6
DILATION_GAP = 2
NODE_BLOCKS = 4
OUTPUT_STEPS = 4
NODES = 2048
BATCH = 8
N_NODE = 4


def draw_tile_src(key, part):
    chosen = jax.random.randint(jax.random.fold_in(key, 11), (N_NODE * N_NODE,), 0, NODE_BLOCKS)
    chosen = chosen.at[0].set(0)
    chosen = chosen.at[1].set(NODE_BLOCKS - 1)
    return chosen.astype(jnp.int32)


def draw_tile_dst(key, part):
    levels = jax.random.randint(jax.random.fold_in(key, 13), (N_NODE, 1), 0, 4)
    coin_flip = jax.random.randint(jax.random.fold_in(key, 17), (N_NODE, N_NODE), 0, 4)
    targets = jax.random.randint(jax.random.fold_in(key, 19), (N_NODE, N_NODE), 0, NODE_BLOCKS)
    sender = lax.broadcasted_iota(jnp.int32, (N_NODE, N_NODE), 0)
    receiver = lax.broadcasted_iota(jnp.int32, (N_NODE, N_NODE), 1)
    first_pair = (sender == 0) & (receiver == 1)
    second_pair = (sender == 1) & (receiver == 0)
    live_slot = (coin_flip <= levels) & (sender != receiver) | first_pair | second_pair
    targets = jnp.where(first_pair, NODE_BLOCKS - 1, targets)
    targets = jnp.where(second_pair, 0, targets)
    return jnp.where(live_slot, targets, -1).reshape(N_NODE * N_NODE).astype(jnp.int32)


def level_of(own_key, dims, split, low, high):
    def one(axis_at, shards_of):
        draws = jax.random.uniform(jax.random.fold_in(jax.random.fold_in(own_key, 6), axis_at), (shards_of,), jnp.float32, low / len(split), high / len(split))
        return jnp.repeat(jnp.exp(draws), dims[axis_at] // shards_of).reshape((-1,) + (1,) * (len(dims) - axis_at - 1))

    loudness = one(*split[0])
    for cut in split[1:]:
        loudness = loudness * one(*cut)
    return loudness


def bell_draw(stream_key, shape, scale, reach, split=(), held_as=jnp.bfloat16):
    array = scale * jax.random.normal(stream_key, shape, jnp.float32)
    if split:
        array = array * level_of(stream_key, shape, split, -0.22, 0.18)
    return jnp.clip(array, -reach, reach).astype(held_as)


def setup_inputs(seed: int = 0) -> dict:
    key_of = jax.random.split(jax.random.key(seed), 16)
    inputs = bell_draw(key_of[0], (BATCH, T_IN, HIDDEN_CHANNELS, NODES), 1.0, 6.0, ((0, 8), (3, 4)))
    w_conv = bell_draw(key_of[1], (2 * HIDDEN_CHANNELS, 2 * HIDDEN_CHANNELS), (2 * HIDDEN_CHANNELS) ** -0.5, 0.5)
    b_conv = bell_draw(key_of[2], (2 * HIDDEN_CHANNELS,), 0.5, 3.0, (), jnp.float32)
    w_mix = bell_draw(key_of[3], (HIDDEN_CHANNELS, 5 * HIDDEN_CHANNELS), (5 * HIDDEN_CHANNELS) ** -0.5, 0.3125)
    b_mix = bell_draw(key_of[4], (HIDDEN_CHANNELS,), 0.5, 3.0, (), jnp.float32)
    w_skip = bell_draw(key_of[5], (SKIP, HIDDEN_CHANNELS), HIDDEN_CHANNELS ** -0.5, 0.75)
    b_skip = bell_draw(key_of[6], (SKIP,), 0.5, 3.0, (), jnp.float32)
    local_fwd = bell_draw(key_of[7], (NODES, 3 * BLOCK), (4 * BLOCK) ** -0.5, 0.25, ((0, 4),))
    local_bwd = bell_draw(key_of[8], (NODES, 3 * BLOCK), (4 * BLOCK) ** -0.5, 0.25, ((0, 4),))
    remote_fwd = bell_draw(key_of[9], (N_NODE * N_NODE, BLOCK, BLOCK), (4 * BLOCK) ** -0.5, 0.25, ((0, 4),))
    remote_bwd = bell_draw(key_of[10], (N_NODE * N_NODE, BLOCK, BLOCK), (4 * BLOCK) ** -0.5, 0.25, ((0, 4),))
    tile_src = draw_tile_src(jax.random.fold_in(key_of[15], 71), 0)
    tile_dst = draw_tile_dst(jax.random.fold_in(key_of[15], 71), 0)
    residual_cotangent = bell_draw(key_of[13], (BATCH, OUTPUT_STEPS, HIDDEN_CHANNELS, NODES), 1.0, 6.0, ((0, 8), (3, 4)))
    cot_skip = bell_draw(key_of[14], (BATCH, SKIP, NODES), 1.0, 6.0, ((0, 8), (2, 4)))
    return {"inputs": inputs, "w_conv": w_conv, "b_conv": b_conv, "w_mix": w_mix, "b_mix": b_mix, "w_skip": w_skip, "b_skip": b_skip, "local_fwd": local_fwd, "local_bwd": local_bwd, "remote_fwd": remote_fwd, "remote_bwd": remote_bwd, "tile_src": tile_src, "tile_dst": tile_dst, "residual_cotangent": residual_cotangent, "cot_skip": cot_skip}


def band_forward(values, weights):
    row_count = values.shape[0]
    shaped = values.astype(jnp.float32).reshape(row_count, N_NODE, NODE_BLOCKS, BLOCK)
    zeros_blk = jnp.zeros((row_count, N_NODE, 1, BLOCK), jnp.float32)
    before = jnp.concatenate([zeros_blk, shaped[:, :, :-1]], axis=2)
    after_blk = jnp.concatenate([shaped[:, :, 1:], zeros_blk], axis=2)
    stacked = jnp.concatenate([before, shaped, after_blk], axis=3)
    shaped_w = weights.astype(jnp.float32).reshape(N_NODE, NODE_BLOCKS, BLOCK, 3 * BLOCK)
    result = jnp.einsum('mpik,piak->mpia', stacked, shaped_w)
    return result.reshape(row_count, NODES)

def band_backward(gradient, weights):
    row_count = gradient.shape[0]
    shaped = gradient.astype(jnp.float32).reshape(row_count, N_NODE, NODE_BLOCKS, BLOCK)
    shaped_w = weights.astype(jnp.float32).reshape(N_NODE, NODE_BLOCKS, BLOCK, 3 * BLOCK)
    spread = jnp.einsum('mpia,piak->mpik', shaped, shaped_w).reshape(row_count, N_NODE, NODE_BLOCKS, 3, BLOCK)
    zeros_blk = jnp.zeros((row_count, N_NODE, 1, BLOCK), jnp.float32)
    from_after = jnp.concatenate([spread[:, :, 1:, 0], zeros_blk], axis=2)
    from_before = jnp.concatenate([zeros_blk, spread[:, :, :-1, 2]], axis=2)
    return (spread[:, :, :, 1] + from_after + from_before).reshape(row_count, NODES)

def chooser(indices):
    block_ids = jnp.arange(NODE_BLOCKS, dtype=jnp.int32)
    return (indices.reshape(N_NODE, N_NODE)[:, :, None] == block_ids[None, None, :]).astype(jnp.float32)

def far_forward(values, tile_vals, src_pick, dst_pick):
    row_count = values.shape[0]
    shaped = values.astype(jnp.float32).reshape(row_count, N_NODE, NODE_BLOCKS, BLOCK)
    picked = jnp.einsum('sqi,msic->sqmc', src_pick, shaped)
    product = jnp.einsum('sqmc,sqac->sqma', picked, tile_vals.astype(jnp.float32).reshape(N_NODE, N_NODE, BLOCK, BLOCK))
    product = lax.optimization_barrier(product.astype(jnp.bfloat16)).astype(jnp.float32)
    result = jnp.einsum('sqi,sqma->mqia', dst_pick, product)
    return result.reshape(row_count, NODES)

def far_backward(operands, src_pick, dst_pick):
    summed = None
    for gradient, tile_vals in operands:
        row_count = gradient.shape[0]
        shaped = gradient.astype(jnp.float32).reshape(row_count, N_NODE, NODE_BLOCKS, BLOCK)
        wanted = jnp.einsum('sqi,mqia->sqma', dst_pick, shaped)
        term = jnp.einsum('sqma,sqac->sqmc', wanted, tile_vals.astype(jnp.float32).reshape(N_NODE, N_NODE, BLOCK, BLOCK))
        summed = term if summed is None else summed + term
    summed = lax.optimization_barrier(summed.astype(jnp.bfloat16)).astype(jnp.float32)
    result = jnp.einsum('sqj,sqmc->msjc', src_pick, summed)
    return result.reshape(row_count, NODES)

def reference(inputs, w_conv, b_conv, w_mix, b_mix, w_skip, b_skip, local_fwd, local_bwd, remote_fwd, remote_bwd, tile_src, tile_dst, residual_cotangent, cot_skip):
    src_pick = chooser(tile_src)
    dst_pick = chooser(tile_dst)
    conv_w = w_conv.astype(jnp.float32)
    mix_w = w_mix.astype(jnp.float32)
    skip_w = w_skip.astype(jnp.float32)
    row_count = OUTPUT_STEPS * HIDDEN_CHANNELS

    def diffuse(values, local_w, remote_w):
        return (band_forward(values, local_w) + far_forward(values, remote_w, src_pick, dst_pick)).astype(jnp.bfloat16)

    def window(carried, slices):
        input_window, res_cot, skip_cot = slices
        paired_taps = jnp.concatenate([input_window[:OUTPUT_STEPS], input_window[DILATION_GAP:]], axis=1).astype(jnp.float32)
        pre_act = jnp.einsum('oc,tcn->ton', conv_w, paired_taps) + b_conv[None, :, None]
        filtered = jnp.tanh(pre_act[:, :HIDDEN_CHANNELS])
        gate_val = jax.nn.sigmoid(pre_act[:, HIDDEN_CHANNELS:])
        hidden = (filtered * gate_val).astype(jnp.bfloat16)
        flat_hidden = hidden.reshape(row_count, NODES)
        hop_fwd = diffuse(flat_hidden, local_fwd, remote_fwd)
        hop_bwd = diffuse(flat_hidden, local_bwd, remote_bwd)
        two_fwd = diffuse(hop_fwd, local_fwd, remote_fwd)
        two_bwd = diffuse(hop_bwd, local_bwd, remote_bwd)
        shape3 = (OUTPUT_STEPS, HIDDEN_CHANNELS, NODES)
        parts = jnp.concatenate([hidden, hop_fwd.reshape(shape3), two_fwd.reshape(shape3), hop_bwd.reshape(shape3), two_bwd.reshape(shape3)], axis=1).astype(jnp.float32)
        mixed_features = jnp.einsum('oc,tcn->ton', mix_w, parts) + b_mix[None, :, None]
        residual_stream = (input_window[DILATION_GAP:].astype(jnp.float32) + mixed_features).astype(jnp.bfloat16)
        last_step = hidden[OUTPUT_STEPS - 1].astype(jnp.float32)
        skip_sum = (jnp.dot(skip_w, last_step) + b_skip[:, None]).astype(jnp.bfloat16)
        residual_float32 = res_cot.astype(jnp.float32)
        skip32 = skip_cot.astype(jnp.float32)
        grad_parts = jnp.einsum('co,tcn->ton', mix_w, residual_float32)

        def group(index):
            return grad_parts[:, index * HIDDEN_CHANNELS:(index + 1) * HIDDEN_CHANNELS].reshape(row_count, NODES)
        back2_fwd = group(2).astype(jnp.bfloat16)
        back2_bwd = group(4).astype(jnp.bfloat16)
        back1_fwd = (group(1) + band_backward(back2_fwd, local_fwd) + far_backward([(back2_fwd, remote_fwd)], src_pick, dst_pick)).astype(jnp.bfloat16)
        back1_bwd = (group(3) + band_backward(back2_bwd, local_bwd) + far_backward([(back2_bwd, remote_bwd)], src_pick, dst_pick)).astype(jnp.bfloat16)
        skip_back = jnp.dot(skip_w.T, skip32)
        direct = grad_parts[:, :HIDDEN_CHANNELS].at[OUTPUT_STEPS - 1].add(skip_back).reshape(row_count, NODES)
        summed = direct + band_backward(back1_fwd, local_fwd) + band_backward(back1_bwd, local_bwd)
        summed = summed + far_backward([(back1_fwd, remote_fwd), (back1_bwd, remote_bwd)], src_pick, dst_pick)
        grad_hidden = summed.astype(jnp.bfloat16).reshape(shape3).astype(jnp.float32)
        grad_pre = jnp.concatenate([grad_hidden * gate_val * (1.0 - filtered * filtered), grad_hidden * filtered * gate_val * (1.0 - gate_val)], axis=1).astype(jnp.bfloat16).astype(jnp.float32)
        tap_gradients = jnp.einsum('oc,ton->tcn', conv_w, grad_pre)
        input_gradient = jnp.zeros((T_IN, HIDDEN_CHANNELS, NODES), jnp.float32)
        input_gradient = input_gradient.at[:OUTPUT_STEPS].add(tap_gradients[:, :HIDDEN_CHANNELS])
        input_gradient = input_gradient.at[DILATION_GAP:].add(tap_gradients[:, HIDDEN_CHANNELS:] + residual_float32)
        updates = (jnp.einsum('ton,tcn->oc', grad_pre, paired_taps), lax.optimization_barrier(jnp.sum(grad_pre, axis=(0, 2))), jnp.einsum('tcn,ton->co', residual_float32, parts), lax.optimization_barrier(jnp.sum(residual_float32, axis=(0, 2))), jnp.dot(skip32, last_step.T), lax.optimization_barrier(jnp.sum(skip32, axis=1)))
        carried = tuple((old + new for old, new in zip(carried, updates)))
        return (carried, (residual_stream, skip_sum, input_gradient.astype(jnp.bfloat16)))
    start = (jnp.zeros((2 * HIDDEN_CHANNELS, 2 * HIDDEN_CHANNELS), jnp.float32), jnp.zeros((2 * HIDDEN_CHANNELS,), jnp.float32), jnp.zeros((HIDDEN_CHANNELS, 5 * HIDDEN_CHANNELS), jnp.float32), jnp.zeros((HIDDEN_CHANNELS,), jnp.float32), jnp.zeros((SKIP, HIDDEN_CHANNELS), jnp.float32), jnp.zeros((SKIP,), jnp.float32))
    totals, outputs = lax.scan(window, start, (inputs, residual_cotangent, cot_skip))
    grad_scale = 1.0 / math.sqrt(float(BATCH * NODES * OUTPUT_STEPS))
    return (outputs[0], outputs[1], outputs[2], totals[0] * grad_scale, totals[1] * grad_scale, totals[2] * grad_scale, totals[3] * grad_scale, totals[4] * grad_scale, totals[5] * grad_scale)
```

```python
import functools
import math

import jax
import jax.numpy as jnp
from jax import lax
from jax.experimental import pallas as pl
from jax.experimental.pallas import tpu as pltpu
from jax.sharding import PartitionSpec as P

DILATION_GAP = 2
MESH = pl.DeviceIdType.MESH
BF16 = jnp.bfloat16
F32 = jnp.float32


def nn(a, b):
    return lax.dot_general(a, b, (((1,), (0,)), ((), ())), preferred_element_type=F32)


def nt(a, b):
    return lax.dot_general(a, b, (((1,), (1,)), ((), ())), preferred_element_type=F32)


def identity(size):
    rows = lax.broadcasted_iota(jnp.int32, (size, size), 0)
    cols = lax.broadcasted_iota(jnp.int32, (size, size), 1)
    return (rows == cols).astype(F32).astype(BF16)


def pick_mask(row, block):
    return (row == block).astype(F32)


def lanes(block, width):
    return slice(block * width, (block + 1) * width)


def kernel(
    sizes,
    x_ref, wc_ref, bc_ref, wm_ref, bm_ref, ws_ref, bs_ref, lf_ref, lb_ref, rf_ref, rb_ref,
    src_ref, dst_ref, rc_ref, cs_ref,
    res_ref, skip_ref, gx_ref, gwc_ref, gbc_ref, gwm_ref, gbm_ref, gws_ref, gbs_ref,
    dense_f, dense_b, hold_f, hold_b, far_f, far_b,
    dst_out, dst_in, tile_in,
    h_out, h_in, rc_out, rc_in, back_out, back_in, two_out, two_in,
    filt, gate, hid, pre, near_f, near_b, base0, base1, base3, mix0, mix1, mix3, hop_f, hop_b,
    one_f, one_b, u_f, u_b,
    early, early_rs, early_node, early_all, late, late_rs, late_node, late_all,
    tile_sem, node_sem, red_sem,
):
    n_node, n_batch, steps, chans, scale = sizes
    width = rf_ref.shape[1]
    blocks = lf_ref.shape[0] // width
    me = lax.axis_index("node")
    row = lax.axis_index("batch")
    offsets = range(1, n_node)
    ahead = [lax.rem(me + r, n_node) for r in offsets]
    behind = [lax.rem(me + n_node - r, n_node) for r in offsets]
    mates = [lax.rem(row + r, n_batch) for r in range(1, n_batch)]

    barrier = pltpu.get_barrier_semaphore()
    for peer in ahead:
        pl.semaphore_signal(barrier, inc=1, device_id={"node": peer}, device_id_type=MESH)
    for peer in mates:
        pl.semaphore_signal(barrier, inc=1, device_id={"batch": peer}, device_id_type=MESH)
    pl.semaphore_wait(barrier, n_node - 1 + n_batch - 1)

    started = []

    def send(src, dst, sems, at, device):
        copy = pltpu.make_async_remote_copy(
            src_ref=src, dst_ref=dst,
            send_sem=sems.at[(0, *at)], recv_sem=sems.at[(1, *at)],
            device_id=device, device_id_type=MESH,
        )
        copy.start()
        started.append(copy)
        return copy

    def step(t):
        return slice(t * chans, (t + 1) * chans)

    id_copies, tile_copies = [], []
    for k, peer in enumerate(ahead):
        dst_out[k] = jnp.full((8, 128), dst_ref[peer], jnp.int32)
        id_copies.append(send(dst_out.at[k], dst_in.at[k], node_sem, (0, k), {"node": peer}))
    for k, peer in enumerate(ahead):
        tile_copies.append(
            (
                send(rf_ref.at[peer], tile_in.at[0, k], tile_sem, (0, k), {"node": peer}),
                send(rb_ref.at[peer], tile_in.at[1, k], tile_sem, (1, k), {"node": peer}),
            )
        )
    src_rows = [jnp.full((1, width), src_ref[peer], jnp.int32) for peer in ahead]

    hid_pick = [[pick_mask(src_rows[k], j).astype(BF16) for j in range(blocks)] for k in range(n_node - 1)]
    bias = jnp.broadcast_to(bc_ref[...], (2 * chans, 2 * chans)).T
    bias = jnp.concatenate([bias] * (blocks * width // (2 * chans)), axis=1)
    taps = [
        jnp.concatenate([x_ref[step(t), :], x_ref[step(t + DILATION_GAP), :]], axis=0)
        for t in range(steps)
    ]
    for t in range(steps):
        act = nn(wc_ref[...], taps[t]) + bias
        f = jnp.tanh(act[:chans])
        s = jax.nn.sigmoid(act[chans:])
        filt[step(t), :] = f
        gate[step(t), :] = s
        hid[step(t), :] = (f * s).astype(BF16)

    h_copies = []
    for k, peer in enumerate(ahead):
        picked = hid[:, lanes(0, width)] * hid_pick[k][0]
        for j in range(1, blocks):
            picked += hid[:, lanes(j, width)] * hid_pick[k][j]
        h_out[k] = picked
        h_copies.append(send(h_out.at[k], h_in.at[k], node_sem, (1, k), {"node": peer}))

    rc_copies = []
    dst_masks = []
    for k, peer in enumerate(behind):
        id_copies[k].wait_recv()
        got = dst_in[k][0:1, :]
        dst_masks.append([pick_mask(got, i) for i in range(blocks)])
        picked = rc_ref[:, lanes(0, width)] * dst_masks[k][0].astype(BF16)
        for i in range(1, blocks):
            picked += rc_ref[:, lanes(i, width)] * dst_masks[k][i].astype(BF16)
        rc_out[k] = picked
        rc_copies.append(send(rc_out.at[k], rc_in.at[k], node_sem, (2, k), {"node": peer}))

    for dense, local in ((dense_f, lf_ref), (dense_b, lb_ref)):
        for i in range(blocks):
            for j in range(blocks):
                o = j - i + 1
                if 0 <= o <= 2:
                    dense[lanes(i, width), lanes(j, width)] = local[lanes(i, width), lanes(o, width)]
                else:
                    dense[lanes(i, width), lanes(j, width)] = jnp.zeros((width, width), BF16)
    for k, peer in enumerate(ahead):
        for hold, tiles in ((hold_f, rf_ref), (hold_b, rb_ref)):
            tile = tiles[peer]
            for j in range(blocks):
                hold[lanes(k, width), lanes(j, width)] = tile * hid_pick[k][j]

    mix_t = nt(identity(5 * chans), wm_ref[...]).astype(BF16)
    conv_t = nt(identity(2 * chans), wc_ref[...]).astype(BF16)
    skip_t = nt(identity(chans), ws_ref[...]).astype(BF16)
    mix_w = [wm_ref[:, lanes(g, chans)] for g in range(5)]

    for t in range(steps):
        cot = rc_ref[step(t), :]
        base0[step(t), :] = nn(mix_t[lanes(0, chans)], cot)
        base1[step(t), :] = nn(mix_t[lanes(1, chans)], cot)
        base3[step(t), :] = nn(mix_t[lanes(3, chans)], cot)
        h_t = hid[step(t), :]
        mix0[step(t), :] = nn(mix_w[0], h_t)
        mix1[step(t), :] = nn(mix_w[1], h_t)
        mix3[step(t), :] = nn(mix_w[3], h_t)
    last = step(steps - 1)
    base0[last, :] += nn(skip_t, cs_ref[...])
    near_f[...] = nn(rc_ref[...], dense_f[...])
    near_b[...] = nn(rc_ref[...], dense_b[...])
    hop_f32 = nt(hid[...], dense_f[...])
    hop_b32 = nt(hid[...], dense_b[...])

    skip = nn(ws_ref[...], hid[last, :])
    half = 128
    for g in range(skip.shape[0] // half):
        part = jnp.broadcast_to(bs_ref[:, lanes(g, half)], (half, half)).T
        part = jnp.concatenate([part] * (blocks * width // half), axis=1)
        skip_ref[lanes(g, half), :] = (skip[lanes(g, half), :] + part).astype(BF16)
    ones = jnp.ones((16, blocks * width), BF16)
    early[...] = jnp.zeros_like(early)
    late[...] = jnp.zeros_like(late)

    for k in range(n_node - 1):
        tile_copies[k][0].wait_recv()
        tile_copies[k][1].wait_recv()
        for i in range(blocks):
            mask = dst_masks[k][i].astype(BF16)
            far_f[lanes(i, width), lanes(k, width)] = tile_in[0, k] * mask
            far_b[lanes(i, width), lanes(k, width)] = tile_in[1, k] * mask

    for copy in h_copies:
        copy.wait_recv()
    far_h = jnp.concatenate([h_in[k] for k in range(n_node - 1)], axis=1)
    hop_f[...] = (hop_f32 + nt(far_h, far_f[...])).astype(BF16)
    hop_b[...] = (hop_b32 + nt(far_h, far_b[...])).astype(BF16)
    for t in range(steps):
        u_f[step(t), :] = (mix1[step(t), :] + nn(mix_w[2], hop_f[step(t), :])).astype(BF16)
        u_b[step(t), :] = (mix3[step(t), :] + nn(mix_w[4], hop_b[step(t), :])).astype(BF16)
    terms = nt(u_f[...], hold_f[...]) + nt(u_b[...], hold_b[...])
    two_copies = []
    for k, peer in enumerate(ahead):
        two_out[k] = terms[:, lanes(k, width)].astype(BF16)
        two_copies.append(send(two_out.at[k], two_in.at[k], node_sem, (3, k), {"node": peer}))

    for copy in rc_copies:
        copy.wait_recv()
    far_rc = jnp.concatenate([rc_in[k] for k in range(n_node - 1)], axis=1)
    r1_f = (near_f[...] + nn(far_rc, hold_f[...])).astype(BF16)
    r1_b = (near_b[...] + nn(far_rc, hold_b[...])).astype(BF16)
    for t in range(steps):
        one_f[step(t), :] = (base1[step(t), :] + nn(mix_t[lanes(2, chans)], r1_f[step(t)])).astype(BF16)
        one_b[step(t), :] = (base3[step(t), :] + nn(mix_t[lanes(4, chans)], r1_b[step(t)])).astype(BF16)
    terms = nn(one_f[...], far_f[...]) + nn(one_b[...], far_b[...])
    back_copies = []
    for k, peer in enumerate(behind):
        back_out[k] = terms[:, lanes(k, width)].astype(BF16)
        back_copies.append(send(back_out.at[k], back_in.at[k], node_sem, (4, k), {"node": peer}))

    def put(buffer, top, value):
        rows = buffer.shape[1]
        value = value.astype(BF16)
        at = top
        while at < top + value.shape[0]:
            c, o = at // rows, at % rows
            n = min(rows - o, top + value.shape[0] - at)
            buffer[c, o : o + n, 0 : value.shape[1]] = value[at - top : at - top + n]
            at += n

    def take(buffer, top, count, cols):
        rows = buffer.shape[1]
        parts = []
        at = top
        while at < top + count:
            c, o = at // rows, at % rows
            n = min(rows - o, top + count - at)
            parts.append(buffer[c, o : o + n, 0:cols].astype(F32))
            at += n
        return parts[0] if len(parts) == 1 else jnp.concatenate(parts, axis=0)

    groups = [None] * 5
    mix_bias = None

    def plus(a, b):
        return b if a is None else a + b

    for t in range(steps):
        cot = rc_ref[step(t), :]
        groups[0] = plus(groups[0], nt(cot, hid[step(t), :]))
        groups[1] = plus(groups[1], nt(cot, hop_f[step(t), :]))
        groups[2] = plus(groups[2], nt(r1_f[step(t)], hop_f[step(t), :]))
        groups[3] = plus(groups[3], nt(cot, hop_b[step(t), :]))
        groups[4] = plus(groups[4], nt(r1_b[step(t)], hop_b[step(t), :]))
        mix_bias = plus(mix_bias, nt(ones, cot))
    skip_grad = nt(cs_ref[...], hid[last, :])
    skip_bias = nt(ones, cs_ref[...])
    skips = skip_grad.shape[0]
    for g in range(5):
        put(early, g * chans, groups[g])
    put(early, 5 * chans, skip_grad)
    bias_top = 5 * chans + skips
    put(early, bias_top, mix_bias)
    for g in range(skips // 128):
        put(early, bias_top + 16 * (g + 1), skip_bias[:, lanes(g, 128)])

    def scatter(buffer, landing, base):
        return [
            send(buffer.at[peer], landing.at[k], red_sem, (base + k,), {"batch": peer})
            for k, peer in enumerate(mates)
        ]

    def across(buffer, landing, nodes, copies, base):
        total = buffer[row].astype(F32)
        for k, copy in enumerate(copies):
            copy.wait_recv()
            total += landing[k].astype(F32)
        nodes[me] = total.astype(BF16)
        return [
            send(nodes.at[me], nodes.at[me], red_sem, (base + k,), {"node": peer})
            for k, peer in enumerate(ahead)
        ]

    def arrived(copies, nodes, sem_base):
        for k, peer in enumerate(behind):
            pltpu.make_async_remote_copy(
                src_ref=nodes.at[peer], dst_ref=nodes.at[peer],
                send_sem=red_sem.at[0, sem_base + k], recv_sem=red_sem.at[1, sem_base + k],
                device_id={"node": peer}, device_id_type=MESH,
            ).wait_recv()

    def gather(nodes, result, base):
        total = nodes[0].astype(F32)
        for k in range(1, n_node):
            total += nodes[k].astype(F32)
        result[row] = total.astype(BF16)
        return [
            send(result.at[row], result.at[row], red_sem, (base + k,), {"batch": peer})
            for k, peer in enumerate(mates)
        ]

    def gathered(result, base):
        for k in range(n_batch - 1):
            peer = lax.rem(row + n_batch - k - 1, n_batch)
            pltpu.make_async_remote_copy(
                src_ref=result.at[peer], dst_ref=result.at[peer],
                send_sem=red_sem.at[0, base + k], recv_sem=red_sem.at[1, base + k],
                device_id={"batch": peer}, device_id_type=MESH,
            ).wait_recv()

    span = 2 * (n_batch - 1) + n_node - 1
    at1, at2 = n_batch - 1, n_batch - 1 + n_node - 1
    early_copies = scatter(early, early_rs, 0)

    near_one = base0[...] + nn(one_f[...], dense_f[...]) + nn(one_b[...], dense_b[...])
    near_u = mix0[...] + nt(u_f[...], dense_f[...]) + nt(u_b[...], dense_b[...])

    early_node_copies = across(early, early_rs, early_node, early_copies, at1)

    for copy in back_copies:
        copy.wait_recv()
    conv_grad = None
    conv_bias = None
    placed = []
    for j in range(blocks):
        total = near_one[:, lanes(j, width)]
        for k in range(n_node - 1):
            total += back_in[k].astype(F32) * pick_mask(src_rows[k], j)
        placed.append(total)
    grad_hidden = jnp.concatenate(placed, axis=1).astype(BF16).astype(F32)
    for t in range(steps):
        f, s, g = filt[step(t), :], gate[step(t), :], grad_hidden[step(t)]
        gs = g * s
        both = jnp.concatenate([gs * (1.0 - f * f), gs * f * (1.0 - s)], axis=0).astype(BF16)
        pre[t] = both
        conv_grad = plus(conv_grad, nt(both, taps[t]))
        conv_bias = plus(conv_bias, nt(ones, both))
    put(late, 0, conv_grad)
    put(late, 2 * chans, conv_bias)
    late_copies = scatter(late, late_rs, span)

    arrived(early_node_copies, early_node, at1)
    gather(early_node, early_all, at2)

    for t in range(steps + DILATION_GAP):
        total = None
        if t < steps:
            total = nn(conv_t[:chans], pre[t])
        if t >= DILATION_GAP:
            total = plus(total, nn(conv_t[chans:], pre[t - DILATION_GAP]))
            total += rc_ref[step(t - DILATION_GAP), :].astype(F32)
        gx_ref[step(t), :] = total.astype(BF16)

    late_node_copies = across(late, late_rs, late_node, late_copies, span + at1)

    for copy in two_copies:
        copy.wait_recv()
    mix_col = jnp.broadcast_to(
        jnp.concatenate([bm_ref[...]] * (128 // chans), axis=1), (128, 128)
    ).T
    mix_col = jnp.concatenate([mix_col[:chans]] * steps, axis=0)
    for i in range(blocks):
        total = near_u[:, lanes(i, width)] + mix_col
        for k in range(n_node - 1):
            total += two_in[k].astype(F32) * dst_masks[k][i]
        total += x_ref[DILATION_GAP * chans :, lanes(i, width)].astype(F32)
        res_ref[:, lanes(i, width)] = total.astype(BF16)

    arrived(late_node_copies, late_node, span + at1)
    gather(late_node, late_all, span + at2)

    gathered(early_all, at2)
    for g in range(5):
        gwm_ref[:, lanes(g, chans)] = take(early_all, g * chans, chans, chans) * scale
    gws_ref[...] = take(early_all, 5 * chans, skips, chans) * scale
    gbm_ref[...] = take(early_all, bias_top, 16, chans)[0:1] * scale
    for g in range(skips // 128):
        gbs_ref[:, lanes(g, 128)] = take(early_all, bias_top + 16 * (g + 1), 16, 128)[0:1] * scale
    gathered(late_all, span + at2)
    gwc_ref[...] = take(late_all, 0, 2 * chans, 2 * chans) * scale
    gbc_ref[...] = take(late_all, 2 * chans, 16, 2 * chans)[0:1] * scale

    for copy in started:
        copy.wait_send()


def shards(
    inputs, w_conv, b_conv, w_mix, b_mix, w_skip, b_skip, local_fwd, local_bwd,
    remote_fwd, remote_bwd, tile_src, tile_dst, residual_cotangent, cot_skip,
):
    n_node, n_batch = lax.axis_size("node"), lax.axis_size("batch")
    windows, input_steps, chans, local_nodes = inputs.shape
    steps = input_steps - DILATION_GAP
    width = remote_fwd.shape[1]
    skips = w_skip.shape[0]
    rows = steps * chans
    scale = 1.0 / math.sqrt(float(windows * n_batch * local_nodes * n_node * steps))
    peers = n_node - 1

    def chunk(total):
        return -(-total // (16 * n_batch)) * 16

    early = chunk(5 * chans + skips + 16 * (1 + skips // 128))
    late = chunk(2 * chans + 16)

    def field(kind):
        return pltpu.VMEM((rows, local_nodes), kind)

    def slots(*shape):
        return pltpu.VMEM((peers, *shape), BF16)

    scratch = (
        [pltpu.VMEM((local_nodes, local_nodes), BF16)] * 2
        + [pltpu.VMEM((peers * width, local_nodes), BF16)] * 2
        + [pltpu.VMEM((local_nodes, peers * width), BF16)] * 2
        + [pltpu.VMEM((peers, 8, 128), jnp.int32)] * 2
        + [pltpu.VMEM((2, peers, width, width), BF16)]
        + [slots(rows, width)] * 8
        + [field(F32), field(F32), field(BF16)]
        + [pltpu.VMEM((steps, 2 * chans, local_nodes), BF16)]
        + [field(F32)] * 8
        + [field(BF16)] * 6
    )
    for size in (early, late):
        scratch += [
            pltpu.VMEM((n_batch, size, 128), BF16),
            pltpu.VMEM((n_batch - 1, size, 128), BF16),
            pltpu.VMEM((n_node, size, 128), BF16),
            pltpu.VMEM((n_batch, size, 128), BF16),
        ]
    scratch += [
        pltpu.SemaphoreType.DMA((2, 2, peers)),
        pltpu.SemaphoreType.DMA((2, 5, peers)),
        pltpu.SemaphoreType.DMA((2, 2 * (2 * (n_batch - 1) + peers))),
    ]
    vmem = pl.BlockSpec(memory_space=pltpu.VMEM)
    smem = pl.BlockSpec(memory_space=pltpu.SMEM)
    results = pl.pallas_call(
        functools.partial(kernel, (n_node, n_batch, steps, chans, scale)),
        out_shape=[
            jax.ShapeDtypeStruct((rows, local_nodes), BF16),
            jax.ShapeDtypeStruct((skips, local_nodes), BF16),
            jax.ShapeDtypeStruct((input_steps * chans, local_nodes), BF16),
            jax.ShapeDtypeStruct((2 * chans, 2 * chans), F32),
            jax.ShapeDtypeStruct((1, 2 * chans), F32),
            jax.ShapeDtypeStruct((chans, 5 * chans), F32),
            jax.ShapeDtypeStruct((1, chans), F32),
            jax.ShapeDtypeStruct((skips, chans), F32),
            jax.ShapeDtypeStruct((1, skips), F32),
        ],
        in_specs=[vmem] * 11 + [smem] * 2 + [vmem] * 2,
        out_specs=[vmem] * 9,
        scratch_shapes=scratch,
        compiler_params=pltpu.CompilerParams(
            collective_id=0, has_side_effects=True, vmem_limit_bytes=56 * 1024 * 1024
        ),
        cost_estimate=pl.CostEstimate(
            flops=2_000_000_000, bytes_accessed=4_000_000, transcendentals=300_000
        ),
    )(
        inputs.reshape(input_steps * chans, local_nodes),
        w_conv, b_conv[None], w_mix, b_mix[None], w_skip, b_skip[None],
        local_fwd, local_bwd, remote_fwd, remote_bwd, tile_src, tile_dst,
        residual_cotangent.reshape(rows, local_nodes),
        cot_skip.reshape(skips, local_nodes),
    )
    res, skip, gx, gwc, gbc, gwm, gbm, gws, gbs = results
    return (
        res.reshape(windows, steps, chans, local_nodes),
        skip.reshape(windows, skips, local_nodes),
        gx.reshape(windows, input_steps, chans, local_nodes),
        gwc, gbc[0], gwm, gbm[0], gws, gbs[0],
    )


def solution(mesh):
    return jax.shard_map(
        shards,
        mesh=mesh,
        in_specs=(
            P("batch", None, None, "node"),
            P(), P(), P(), P(), P(), P(),
            P("node", None),
            P("node", None),
            P("node", None, None),
            P("node", None, None),
            P("node"),
            P("node"),
            P("batch", None, None, "node"),
            P("batch", None, "node"),
        ),
        out_specs=(
            P("batch", None, None, "node"),
            P("batch", None, "node"),
            P("batch", None, None, "node"),
            P(), P(), P(), P(), P(), P(),
        ),
        check_vma=False,
    )
```

```python
import functools
import math

import jax
import jax.numpy as jnp
from jax import lax
from jax.experimental import pallas as pl
from jax.experimental.pallas import tpu as pltpu
from jax.sharding import PartitionSpec as P

DILATION_GAP = 2
MESH = pl.DeviceIdType.MESH
BF16 = jnp.bfloat16
F32 = jnp.float32


def nn(a, b):
    return lax.dot_general(a, b, (((1,), (0,)), ((), ())), preferred_element_type=F32)


def nt(a, b):
    return lax.dot_general(a, b, (((1,), (1,)), ((), ())), preferred_element_type=F32)


def identity(size):
    rows = lax.broadcasted_iota(jnp.int32, (size, size), 0)
    cols = lax.broadcasted_iota(jnp.int32, (size, size), 1)
    return (rows == cols).astype(F32).astype(BF16)


def pick_mask(row, block):
    return (row == block).astype(F32)


def lanes(block, width):
    return slice(block * width, (block + 1) * width)


def kernel(
    sizes,
    x_ref, wc_ref, bc_ref, wm_ref, bm_ref, ws_ref, bs_ref, lf_ref, lb_ref, rf_ref, rb_ref,
    src_ref, dst_ref, rc_ref, cs_ref,
    res_ref, skip_ref, gx_ref, early_ref, late_ref,
    dense_f, dense_b, hold_f, hold_b, far_f, far_b,
    dst_out, dst_in, tile_in,
    h_out, h_in, rc_out, rc_in, back_out, back_in, two_out, two_in,
    filt, gate, hid, pre, near_f, near_b, base0, base1, base3, mix0, mix1, mix3, hop_f, hop_b,
    one_f, one_b, u_f, u_b,
    early, early_rs, early_node, early_all, late, late_rs, late_node, late_all,
    tile_sem, node_sem, red_sem,
):
    n_node, n_batch, steps, chans, scale = sizes
    width = rf_ref.shape[1]
    blocks = lf_ref.shape[0] // width
    me = lax.axis_index("node")
    row = lax.axis_index("batch")
    offsets = range(1, n_node)
    ahead = [lax.rem(me + r, n_node) for r in offsets]
    behind = [lax.rem(me + n_node - r, n_node) for r in offsets]
    mates = [lax.rem(row + r, n_batch) for r in range(1, n_batch)]

    barrier = pltpu.get_barrier_semaphore()
    for peer in ahead:
        pl.semaphore_signal(barrier, inc=1, device_id={"node": peer}, device_id_type=MESH)
    for peer in mates:
        pl.semaphore_signal(barrier, inc=1, device_id={"batch": peer}, device_id_type=MESH)
    pl.semaphore_wait(barrier, n_node - 1 + n_batch - 1)

    started = []

    def send(src, dst, sems, at, device):
        copy = pltpu.make_async_remote_copy(
            src_ref=src, dst_ref=dst,
            send_sem=sems.at[(0, *at)], recv_sem=sems.at[(1, *at)],
            device_id=device, device_id_type=MESH,
        )
        copy.start()
        started.append(copy)
        return copy

    def step(t):
        return slice(t * chans, (t + 1) * chans)

    id_copies, tile_copies = [], []
    for k, peer in enumerate(ahead):
        dst_out[k] = jnp.full((8, 128), dst_ref[peer], jnp.int32)
        id_copies.append(send(dst_out.at[k], dst_in.at[k], node_sem, (0, k), {"node": peer}))
    for k, peer in enumerate(ahead):
        tile_copies.append(
            (
                send(rf_ref.at[peer], tile_in.at[0, k], tile_sem, (0, k), {"node": peer}),
                send(rb_ref.at[peer], tile_in.at[1, k], tile_sem, (1, k), {"node": peer}),
            )
        )
    src_rows = [jnp.full((1, width), src_ref[peer], jnp.int32) for peer in ahead]

    hid_pick = [[pick_mask(src_rows[k], j).astype(BF16) for j in range(blocks)] for k in range(n_node - 1)]
    bias = jnp.broadcast_to(bc_ref[...], (2 * chans, 2 * chans)).T
    bias = jnp.concatenate([bias] * (blocks * width // (2 * chans)), axis=1)
    taps = [
        jnp.concatenate([x_ref[step(t), :], x_ref[step(t + DILATION_GAP), :]], axis=0)
        for t in range(steps)
    ]
    for t in range(steps):
        act = nn(wc_ref[...], taps[t]) + bias
        f = jnp.tanh(act[:chans])
        s = jax.nn.sigmoid(act[chans:])
        filt[step(t), :] = f
        gate[step(t), :] = s
        hid[step(t), :] = (f * s).astype(BF16)

    h_copies = []
    for k, peer in enumerate(ahead):
        picked = hid[:, lanes(0, width)] * hid_pick[k][0]
        for j in range(1, blocks):
            picked += hid[:, lanes(j, width)] * hid_pick[k][j]
        h_out[k] = picked
        h_copies.append(send(h_out.at[k], h_in.at[k], node_sem, (1, k), {"node": peer}))

    rc_copies = []
    dst_masks = []
    for k, peer in enumerate(behind):
        id_copies[k].wait_recv()
        got = dst_in[k][0:1, :]
        dst_masks.append([pick_mask(got, i) for i in range(blocks)])
        picked = rc_ref[:, lanes(0, width)] * dst_masks[k][0].astype(BF16)
        for i in range(1, blocks):
            picked += rc_ref[:, lanes(i, width)] * dst_masks[k][i].astype(BF16)
        rc_out[k] = picked
        rc_copies.append(send(rc_out.at[k], rc_in.at[k], node_sem, (2, k), {"node": peer}))

    for dense, local in ((dense_f, lf_ref), (dense_b, lb_ref)):
        for i in range(blocks):
            for j in range(blocks):
                o = j - i + 1
                if 0 <= o <= 2:
                    dense[lanes(i, width), lanes(j, width)] = local[lanes(i, width), lanes(o, width)]
                else:
                    dense[lanes(i, width), lanes(j, width)] = jnp.zeros((width, width), BF16)
    for k, peer in enumerate(ahead):
        for hold, tiles in ((hold_f, rf_ref), (hold_b, rb_ref)):
            tile = tiles[peer]
            for j in range(blocks):
                hold[lanes(k, width), lanes(j, width)] = tile * hid_pick[k][j]

    mix_t = nt(identity(5 * chans), wm_ref[...]).astype(BF16)
    conv_t = nt(identity(2 * chans), wc_ref[...]).astype(BF16)
    skips = ws_ref.shape[1]
    skip_w = nt(identity(skips), ws_ref[...]).astype(BF16)
    mix_w = [wm_ref[:, lanes(g, chans)] for g in range(5)]

    for t in range(steps):
        cot = rc_ref[step(t), :]
        base0[step(t), :] = nn(mix_t[lanes(0, chans)], cot)
        base1[step(t), :] = nn(mix_t[lanes(1, chans)], cot)
        base3[step(t), :] = nn(mix_t[lanes(3, chans)], cot)
        h_t = hid[step(t), :]
        mix0[step(t), :] = nn(mix_w[0], h_t)
        mix1[step(t), :] = nn(mix_w[1], h_t)
        mix3[step(t), :] = nn(mix_w[3], h_t)
    last = step(steps - 1)
    base0[last, :] += nn(ws_ref[...], cs_ref[...])
    near_f[...] = nn(rc_ref[...], dense_f[...])
    near_b[...] = nn(rc_ref[...], dense_b[...])
    hop_f32 = nt(hid[...], dense_f[...])
    hop_b32 = nt(hid[...], dense_b[...])

    skip = nn(skip_w, hid[last, :])
    half = 128
    for g in range(skip.shape[0] // half):
        part = jnp.broadcast_to(bs_ref[:, lanes(g, half)], (half, half)).T
        part = jnp.concatenate([part] * (blocks * width // half), axis=1)
        skip_ref[lanes(g, half), :] = (skip[lanes(g, half), :] + part).astype(BF16)
    ones = jnp.ones((16, blocks * width), BF16)
    early[...] = jnp.zeros_like(early)
    late[...] = jnp.zeros_like(late)

    for k in range(n_node - 1):
        tile_copies[k][0].wait_recv()
        tile_copies[k][1].wait_recv()
        for i in range(blocks):
            mask = dst_masks[k][i].astype(BF16)
            far_f[lanes(i, width), lanes(k, width)] = tile_in[0, k] * mask
            far_b[lanes(i, width), lanes(k, width)] = tile_in[1, k] * mask

    for copy in h_copies:
        copy.wait_recv()
    far_h = jnp.concatenate([h_in[k] for k in range(n_node - 1)], axis=1)
    hop_f[...] = (hop_f32 + nt(far_h, far_f[...])).astype(BF16)
    hop_b[...] = (hop_b32 + nt(far_h, far_b[...])).astype(BF16)
    for t in range(steps):
        u_f[step(t), :] = (mix1[step(t), :] + nn(mix_w[2], hop_f[step(t), :])).astype(BF16)
        u_b[step(t), :] = (mix3[step(t), :] + nn(mix_w[4], hop_b[step(t), :])).astype(BF16)
    terms = nt(u_f[...], hold_f[...]) + nt(u_b[...], hold_b[...])
    two_copies = []
    for k, peer in enumerate(ahead):
        two_out[k] = terms[:, lanes(k, width)].astype(BF16)
        two_copies.append(send(two_out.at[k], two_in.at[k], node_sem, (3, k), {"node": peer}))

    for copy in rc_copies:
        copy.wait_recv()
    far_rc = jnp.concatenate([rc_in[k] for k in range(n_node - 1)], axis=1)
    r1_f = (near_f[...] + nn(far_rc, hold_f[...])).astype(BF16)
    r1_b = (near_b[...] + nn(far_rc, hold_b[...])).astype(BF16)
    for t in range(steps):
        one_f[step(t), :] = (base1[step(t), :] + nn(mix_t[lanes(2, chans)], r1_f[step(t)])).astype(BF16)
        one_b[step(t), :] = (base3[step(t), :] + nn(mix_t[lanes(4, chans)], r1_b[step(t)])).astype(BF16)
    terms = nn(one_f[...], far_f[...]) + nn(one_b[...], far_b[...])
    back_copies = []
    for k, peer in enumerate(behind):
        back_out[k] = terms[:, lanes(k, width)].astype(BF16)
        back_copies.append(send(back_out.at[k], back_in.at[k], node_sem, (4, k), {"node": peer}))

    def put(buffer, top, value):
        rows = buffer.shape[1]
        value = value.astype(BF16)
        at = top
        while at < top + value.shape[0]:
            c, o = at // rows, at % rows
            n = min(rows - o, top + value.shape[0] - at)
            buffer[c, o : o + n, 0 : value.shape[1]] = value[at - top : at - top + n]
            at += n

    groups = [None] * 5
    mix_bias = None

    def plus(a, b):
        return b if a is None else a + b

    for t in range(steps):
        cot = rc_ref[step(t), :]
        groups[0] = plus(groups[0], nt(cot, hid[step(t), :]))
        groups[1] = plus(groups[1], nt(cot, hop_f[step(t), :]))
        groups[2] = plus(groups[2], nt(r1_f[step(t)], hop_f[step(t), :]))
        groups[3] = plus(groups[3], nt(cot, hop_b[step(t), :]))
        groups[4] = plus(groups[4], nt(r1_b[step(t)], hop_b[step(t), :]))
        mix_bias = plus(mix_bias, nt(ones, cot))
    skip_grad = nt(hid[last, :], cs_ref[...])
    skip_bias = nt(ones, cs_ref[...])
    put(early, 0, jnp.concatenate([groups[0], groups[1]], axis=1))
    put(early, chans, jnp.concatenate([groups[2], groups[3]], axis=1))
    put(early, 2 * chans, groups[4])
    bias_top = 3 * chans
    put(early, bias_top, mix_bias)
    for g in range(skips // 128):
        put(early, bias_top + 16 * (g + 1), skip_bias[:, lanes(g, 128)])
    skip_top = bias_top + 16 * (1 + skips // 128)
    for g in range(skips // 128):
        put(early, skip_top + g * chans, skip_grad[:, lanes(g, 128)])

    def scatter(buffer, landing, base):
        return [
            send(buffer.at[peer], landing.at[k], red_sem, (base + k,), {"batch": peer})
            for k, peer in enumerate(mates)
        ]

    def across(buffer, landing, nodes, copies, base):
        total = buffer[row].astype(F32)
        for k, copy in enumerate(copies):
            copy.wait_recv()
            total += landing[k].astype(F32)
        nodes[me] = total.astype(BF16)
        return [
            send(nodes.at[me], nodes.at[me], red_sem, (base + k,), {"node": peer})
            for k, peer in enumerate(ahead)
        ]

    def arrived(copies, nodes, sem_base):
        for k, peer in enumerate(behind):
            pltpu.make_async_remote_copy(
                src_ref=nodes.at[peer], dst_ref=nodes.at[peer],
                send_sem=red_sem.at[0, sem_base + k], recv_sem=red_sem.at[1, sem_base + k],
                device_id={"node": peer}, device_id_type=MESH,
            ).wait_recv()

    def gather(nodes, result, base):
        total = nodes[0].astype(F32)
        for k in range(1, n_node):
            total += nodes[k].astype(F32)
        result[row] = total.astype(BF16)
        return [
            send(result.at[row], result.at[row], red_sem, (base + k,), {"batch": peer})
            for k, peer in enumerate(mates)
        ]

    def gathered(result, base):
        for k in range(n_batch - 1):
            peer = lax.rem(row + n_batch - k - 1, n_batch)
            pltpu.make_async_remote_copy(
                src_ref=result.at[peer], dst_ref=result.at[peer],
                send_sem=red_sem.at[0, base + k], recv_sem=red_sem.at[1, base + k],
                device_id={"batch": peer}, device_id_type=MESH,
            ).wait_recv()

    span = 2 * (n_batch - 1) + n_node - 1
    at1, at2 = n_batch - 1, n_batch - 1 + n_node - 1
    early_copies = scatter(early, early_rs, 0)

    near_one = base0[...] + nn(one_f[...], dense_f[...]) + nn(one_b[...], dense_b[...])
    near_u = mix0[...] + nt(u_f[...], dense_f[...]) + nt(u_b[...], dense_b[...])

    early_node_copies = across(early, early_rs, early_node, early_copies, at1)

    for copy in back_copies:
        copy.wait_recv()
    conv_grad = None
    conv_bias = None
    placed = []
    for j in range(blocks):
        total = near_one[:, lanes(j, width)]
        for k in range(n_node - 1):
            total += back_in[k].astype(F32) * pick_mask(src_rows[k], j)
        placed.append(total)
    grad_hidden = jnp.concatenate(placed, axis=1).astype(BF16).astype(F32)
    for t in range(steps):
        f, s, g = filt[step(t), :], gate[step(t), :], grad_hidden[step(t)]
        gs = g * s
        both = jnp.concatenate([gs * (1.0 - f * f), gs * f * (1.0 - s)], axis=0).astype(BF16)
        pre[t] = both
        conv_grad = plus(conv_grad, nt(both, taps[t]))
        conv_bias = plus(conv_bias, nt(ones, both))
    put(late, 0, conv_grad)
    put(late, 2 * chans, conv_bias)
    late_copies = scatter(late, late_rs, span)

    arrived(early_node_copies, early_node, at1)
    gather(early_node, early_all, at2)

    for t in range(steps + DILATION_GAP):
        total = None
        if t < steps:
            total = nn(conv_t[:chans], pre[t])
        if t >= DILATION_GAP:
            total = plus(total, nn(conv_t[chans:], pre[t - DILATION_GAP]))
            total += rc_ref[step(t - DILATION_GAP), :].astype(F32)
        gx_ref[step(t), :] = total.astype(BF16)

    late_node_copies = across(late, late_rs, late_node, late_copies, span + at1)

    for copy in two_copies:
        copy.wait_recv()
    mix_col = jnp.broadcast_to(
        jnp.concatenate([bm_ref[...]] * (128 // chans), axis=1), (128, 128)
    ).T
    mix_col = jnp.concatenate([mix_col[:chans]] * steps, axis=0)
    for i in range(blocks):
        total = near_u[:, lanes(i, width)] + mix_col
        for k in range(n_node - 1):
            total += two_in[k].astype(F32) * dst_masks[k][i]
        total += x_ref[DILATION_GAP * chans :, lanes(i, width)].astype(F32)
        res_ref[:, lanes(i, width)] = total.astype(BF16)

    arrived(late_node_copies, late_node, span + at1)
    gather(late_node, late_all, span + at2)

    gathered(early_all, at2)
    early_ref[...] = early_all[...]
    gathered(late_all, span + at2)
    late_ref[...] = late_all[...]

    for copy in started:
        copy.wait_send()


def finish(
    sizes, res_in, skip_in, gx_in, early, late,
    res_ref, skip_ref, gx_ref, gwc_ref, gbc_ref, gwm_ref, gbm_ref, gws_ref, gbs_ref, sems,
):
    chans, skips, scale = sizes
    copies = [
        pltpu.make_async_copy(a, b, sems.at[k])
        for k, (a, b) in enumerate(((res_in, res_ref), (skip_in, skip_ref), (gx_in, gx_ref)))
    ]
    for copy in copies:
        copy.start()

    def take(buffer, top, count):
        rows = buffer.shape[1]
        parts = []
        at = top
        while at < top + count:
            c, o = at // rows, at % rows
            n = min(rows - o, top + count - at)
            parts.append(buffer[c, o : o + n, :].astype(F32))
            at += n
        return (parts[0] if len(parts) == 1 else jnp.concatenate(parts, axis=0)) * scale

    gwm_ref[:, : 2 * chans] = take(early, 0, chans)
    gwm_ref[:, 2 * chans : 4 * chans] = take(early, chans, chans)
    gwm_ref[:, 4 * chans :] = take(early, 2 * chans, chans)[:, :chans]
    bias_top = 3 * chans
    gbm_ref[...] = take(early, bias_top, 16)[0:1, :chans]
    skip_top = bias_top + 16 * (1 + skips // 128)
    for g in range(skips // 128):
        gbs_ref[:, lanes(g, 128)] = take(early, bias_top + 16 * (g + 1), 16)[0:1]
        gws_ref[:, lanes(g, 128)] = take(early, skip_top + g * chans, chans)
    gwc_ref[...] = take(late, 0, 2 * chans)
    gbc_ref[...] = take(late, 2 * chans, 16)[0:1]
    for copy in copies:
        copy.wait()


def shards(
    inputs, w_conv, b_conv, w_mix, b_mix, w_skip, b_skip, local_fwd, local_bwd,
    remote_fwd, remote_bwd, tile_src, tile_dst, residual_cotangent, cot_skip,
):
    n_node, n_batch = lax.axis_size("node"), lax.axis_size("batch")
    windows, input_steps, chans, local_nodes = inputs.shape
    steps = input_steps - DILATION_GAP
    width = remote_fwd.shape[1]
    skips = w_skip.shape[0]
    rows = steps * chans
    scale = 1.0 / math.sqrt(float(windows * n_batch * local_nodes * n_node * steps))
    peers = n_node - 1

    def chunk(total):
        return -(-total // (16 * n_batch)) * 16

    early = chunk(3 * chans + 16 * (1 + skips // 128) + skips // 128 * chans)
    late = chunk(2 * chans + 16)

    def field(kind):
        return pltpu.VMEM((rows, local_nodes), kind)

    def slots(*shape):
        return pltpu.VMEM((peers, *shape), BF16)

    scratch = (
        [pltpu.VMEM((local_nodes, local_nodes), BF16)] * 2
        + [pltpu.VMEM((peers * width, local_nodes), BF16)] * 2
        + [pltpu.VMEM((local_nodes, peers * width), BF16)] * 2
        + [pltpu.VMEM((peers, 8, 128), jnp.int32)] * 2
        + [pltpu.VMEM((2, peers, width, width), BF16)]
        + [slots(rows, width)] * 8
        + [field(F32), field(F32), field(BF16)]
        + [pltpu.VMEM((steps, 2 * chans, local_nodes), BF16)]
        + [field(F32)] * 8
        + [field(BF16)] * 6
    )
    for size in (early, late):
        scratch += [
            pltpu.VMEM((n_batch, size, 128), BF16),
            pltpu.VMEM((n_batch - 1, size, 128), BF16),
            pltpu.VMEM((n_node, size, 128), BF16),
            pltpu.VMEM((n_batch, size, 128), BF16),
        ]
    scratch += [
        pltpu.SemaphoreType.DMA((2, 2, peers)),
        pltpu.SemaphoreType.DMA((2, 5, peers)),
        pltpu.SemaphoreType.DMA((2, 2 * (2 * (n_batch - 1) + peers))),
    ]
    vmem = pl.BlockSpec(memory_space=pltpu.VMEM)
    smem = pl.BlockSpec(memory_space=pltpu.SMEM)
    results = pl.pallas_call(
        functools.partial(kernel, (n_node, n_batch, steps, chans, scale)),
        out_shape=[
            jax.ShapeDtypeStruct((rows, local_nodes), BF16),
            jax.ShapeDtypeStruct((skips, local_nodes), BF16),
            jax.ShapeDtypeStruct((input_steps * chans, local_nodes), BF16),
            jax.ShapeDtypeStruct((n_batch, early, 128), BF16),
            jax.ShapeDtypeStruct((n_batch, late, 128), BF16),
        ],
        in_specs=[vmem] * 11 + [smem] * 2 + [vmem] * 2,
        out_specs=[vmem] * 5,
        scratch_shapes=scratch,
        compiler_params=pltpu.CompilerParams(
            collective_id=0, has_side_effects=True, vmem_limit_bytes=56 * 1024 * 1024
        ),
        cost_estimate=pl.CostEstimate(
            flops=2_000_000_000, bytes_accessed=4_000_000, transcendentals=300_000
        ),
    )(
        inputs.reshape(input_steps * chans, local_nodes),
        w_conv, b_conv[None], w_mix, b_mix[None], w_skip.T, b_skip[None],
        local_fwd, local_bwd, remote_fwd, remote_bwd, tile_src, tile_dst,
        residual_cotangent.reshape(rows, local_nodes),
        cot_skip.reshape(skips, local_nodes),
    )
    anywhere = pl.BlockSpec(memory_space=pl.ANY)
    res, skip, gx, gwc, gbc, gwm, gbm, gws, gbs = pl.pallas_call(
        functools.partial(finish, (chans, skips, scale)),
        out_shape=[
            *[jax.ShapeDtypeStruct(a.shape, a.dtype) for a in results[:3]],
            jax.ShapeDtypeStruct((2 * chans, 2 * chans), F32),
            jax.ShapeDtypeStruct((1, 2 * chans), F32),
            jax.ShapeDtypeStruct((chans, 5 * chans), F32),
            jax.ShapeDtypeStruct((1, chans), F32),
            jax.ShapeDtypeStruct((chans, skips), F32),
            jax.ShapeDtypeStruct((1, skips), F32),
        ],
        in_specs=[anywhere] * 3 + [vmem] * 2,
        out_specs=[anywhere] * 3 + [vmem] * 6,
        scratch_shapes=[pltpu.SemaphoreType.DMA((3,))],
        compiler_params=pltpu.CompilerParams(vmem_limit_bytes=56 * 1024 * 1024),
    )(*results)
    return (
        res.reshape(windows, steps, chans, local_nodes),
        skip.reshape(windows, skips, local_nodes),
        gx.reshape(windows, input_steps, chans, local_nodes),
        gwc, gbc[0], gwm, gbm[0], gws.T, gbs[0],
    )


def solution(mesh):
    return jax.shard_map(
        shards,
        mesh=mesh,
        in_specs=(
            P("batch", None, None, "node"),
            P(), P(), P(), P(), P(), P(),
            P("node", None),
            P("node", None),
            P("node", None, None),
            P("node", None, None),
            P("node"),
            P("node"),
            P("batch", None, None, "node"),
            P("batch", None, "node"),
        ),
        out_specs=(
            P("batch", None, None, "node"),
            P("batch", None, "node"),
            P("batch", None, None, "node"),
            P(), P(), P(), P(), P(), P(),
        ),
        check_vma=False,
    )
```

```python
import functools
import math

import jax
import jax.numpy as jnp
from jax import lax
from jax.experimental import pallas as pl
from jax.experimental.pallas import tpu as pltpu
from jax.sharding import PartitionSpec as P

DILATION_GAP = 2
MESH = pl.DeviceIdType.MESH
BF16 = jnp.bfloat16
F32 = jnp.float32


def nn(a, b):
    return lax.dot_general(a, b, (((1,), (0,)), ((), ())), preferred_element_type=F32)


def nt(a, b):
    return lax.dot_general(a, b, (((1,), (1,)), ((), ())), preferred_element_type=F32)


def identity(size):
    rows = lax.broadcasted_iota(jnp.int32, (size, size), 0)
    cols = lax.broadcasted_iota(jnp.int32, (size, size), 1)
    return (rows == cols).astype(F32).astype(BF16)


def pick_mask(row, block):
    return (row == block).astype(F32)


def lanes(block, width):
    return slice(block * width, (block + 1) * width)


def kernel(
    sizes,
    x_ref, wc_ref, bc_ref, wm_ref, bm_ref, ws_ref, bs_ref, lf_ref, lb_ref, rf_ref, rb_ref,
    src_ref, dst_ref, rc_ref, cs_ref,
    res_ref, skip_ref, gx_ref, early_ref, late_ref,
    dense_f, dense_b, hold_f, hold_b, far_f, far_b,
    dst_out, dst_in, tile_in,
    h_out, h_in, rc_out, rc_in, back_out, back_in, two_out, two_in,
    filt, gate, hid, pre, near_f, near_b, base0, base1, base3, mix0, mix1, mix3, hop_f, hop_b,
    one_f, one_b, u_f, u_b,
    early, early_rs, early_node, early_all, late, late_rs, late_node, late_all,
    tile_sem, node_sem, red_sem,
):
    n_node, n_batch, steps, chans, scale = sizes
    width = rf_ref.shape[1]
    blocks = lf_ref.shape[0] // width
    me = lax.axis_index("node")
    row = lax.axis_index("batch")
    offsets = range(1, n_node)
    ahead = behind = [me ^ r for r in offsets]
    mates = [lax.rem(row + r, n_batch) for r in range(1, n_batch)]

    barrier = pltpu.get_barrier_semaphore()
    for peer in ahead:
        pl.semaphore_signal(barrier, inc=1, device_id={"node": peer}, device_id_type=MESH)
    for peer in mates:
        pl.semaphore_signal(barrier, inc=1, device_id={"batch": peer}, device_id_type=MESH)
    pl.semaphore_wait(barrier, n_node - 1 + n_batch - 1)

    started = []

    def send(src, dst, sems, at, device):
        copy = pltpu.make_async_remote_copy(
            src_ref=src, dst_ref=dst,
            send_sem=sems.at[(0, *at)], recv_sem=sems.at[(1, *at)],
            device_id=device, device_id_type=MESH,
        )
        copy.start()
        started.append(copy)
        return copy

    def step(t):
        return slice(t * chans, (t + 1) * chans)

    id_copies, tile_copies = [], []
    for k, peer in enumerate(ahead):
        dst_out[k] = jnp.full((8, 128), dst_ref[peer], jnp.int32)
        id_copies.append(send(dst_out.at[k], dst_in.at[k], node_sem, (0, k), {"node": peer}))
    for k, peer in enumerate(ahead):
        tile_copies.append(
            (
                send(rf_ref.at[peer], tile_in.at[0, k], tile_sem, (0, k), {"node": peer}),
                send(rb_ref.at[peer], tile_in.at[1, k], tile_sem, (1, k), {"node": peer}),
            )
        )
    src_rows = [jnp.full((1, width), src_ref[peer], jnp.int32) for peer in ahead]

    rc_copies = []
    dst_masks = []
    for k, peer in enumerate(behind):
        id_copies[k].wait_recv()
        got = dst_in[k][0:1, :]
        dst_masks.append([pick_mask(got, i) for i in range(blocks)])
        picked = rc_ref[:, lanes(0, width)] * dst_masks[k][0].astype(BF16)
        for i in range(1, blocks):
            picked += rc_ref[:, lanes(i, width)] * dst_masks[k][i].astype(BF16)
        rc_out[k] = picked
        rc_copies.append(send(rc_out.at[k], rc_in.at[k], node_sem, (2, k), {"node": peer}))

    hid_pick = [[pick_mask(src_rows[k], j).astype(BF16) for j in range(blocks)] for k in range(n_node - 1)]
    bias = jnp.broadcast_to(bc_ref[...], (2 * chans, 2 * chans)).T
    bias = jnp.concatenate([bias] * (blocks * width // (2 * chans)), axis=1)
    taps = [
        jnp.concatenate([x_ref[step(t), :], x_ref[step(t + DILATION_GAP), :]], axis=0)
        for t in range(steps)
    ]
    for t in range(steps):
        act = nn(wc_ref[...], taps[t]) + bias
        f = jnp.tanh(act[:chans])
        s = jax.nn.sigmoid(act[chans:])
        filt[step(t), :] = f
        gate[step(t), :] = s
        hid[step(t), :] = (f * s).astype(BF16)

    h_copies = []
    for k, peer in enumerate(ahead):
        picked = hid[:, lanes(0, width)] * hid_pick[k][0]
        for j in range(1, blocks):
            picked += hid[:, lanes(j, width)] * hid_pick[k][j]
        h_out[k] = picked
        h_copies.append(send(h_out.at[k], h_in.at[k], node_sem, (1, k), {"node": peer}))

    for dense, local in ((dense_f, lf_ref), (dense_b, lb_ref)):
        for i in range(blocks):
            for j in range(blocks):
                o = j - i + 1
                if 0 <= o <= 2:
                    dense[lanes(i, width), lanes(j, width)] = local[lanes(i, width), lanes(o, width)]
                else:
                    dense[lanes(i, width), lanes(j, width)] = jnp.zeros((width, width), BF16)
    for k, peer in enumerate(ahead):
        for hold, tiles in ((hold_f, rf_ref), (hold_b, rb_ref)):
            tile = tiles[peer]
            for j in range(blocks):
                hold[lanes(k, width), lanes(j, width)] = tile * hid_pick[k][j]

    mix_t = nt(identity(5 * chans), wm_ref[...]).astype(BF16)
    conv_t = nt(identity(2 * chans), wc_ref[...]).astype(BF16)
    skips = ws_ref.shape[1]
    skip_w = nt(identity(skips), ws_ref[...]).astype(BF16)
    mix_w = [wm_ref[:, lanes(g, chans)] for g in range(5)]

    for t in range(steps):
        cot = rc_ref[step(t), :]
        base1[step(t), :] = nn(mix_t[lanes(1, chans)], cot)
        base3[step(t), :] = nn(mix_t[lanes(3, chans)], cot)
    near_f[...] = nn(rc_ref[...], dense_f[...])
    near_b[...] = nn(rc_ref[...], dense_b[...])

    for k in range(n_node - 1):
        tile_copies[k][0].wait_recv()
        tile_copies[k][1].wait_recv()
        for i in range(blocks):
            mask = dst_masks[k][i].astype(BF16)
            far_f[lanes(i, width), lanes(k, width)] = tile_in[0, k] * mask
            far_b[lanes(i, width), lanes(k, width)] = tile_in[1, k] * mask

    for copy in rc_copies:
        copy.wait_recv()
    far_rc = jnp.concatenate([rc_in[k] for k in range(n_node - 1)], axis=1)
    r1_f = (near_f[...] + nn(far_rc, hold_f[...])).astype(BF16)
    r1_b = (near_b[...] + nn(far_rc, hold_b[...])).astype(BF16)
    for t in range(steps):
        one_f[step(t), :] = (base1[step(t), :] + nn(mix_t[lanes(2, chans)], r1_f[step(t)])).astype(BF16)
        one_b[step(t), :] = (base3[step(t), :] + nn(mix_t[lanes(4, chans)], r1_b[step(t)])).astype(BF16)
    terms = nn(one_f[...], far_f[...]) + nn(one_b[...], far_b[...])
    back_copies = []
    for k, peer in enumerate(behind):
        back_out[k] = terms[:, lanes(k, width)].astype(BF16)
        back_copies.append(send(back_out.at[k], back_in.at[k], node_sem, (4, k), {"node": peer}))

    for t in range(steps):
        h_t = hid[step(t), :]
        mix1[step(t), :] = nn(mix_w[1], h_t)
        mix3[step(t), :] = nn(mix_w[3], h_t)
    hop_f32 = nt(hid[...], dense_f[...])
    hop_b32 = nt(hid[...], dense_b[...])

    for copy in h_copies:
        copy.wait_recv()
    far_h = jnp.concatenate([h_in[k] for k in range(n_node - 1)], axis=1)
    hop_f[...] = (hop_f32 + nt(far_h, far_f[...])).astype(BF16)
    hop_b[...] = (hop_b32 + nt(far_h, far_b[...])).astype(BF16)
    for t in range(steps):
        u_f[step(t), :] = (mix1[step(t), :] + nn(mix_w[2], hop_f[step(t), :])).astype(BF16)
        u_b[step(t), :] = (mix3[step(t), :] + nn(mix_w[4], hop_b[step(t), :])).astype(BF16)
    terms = nt(u_f[...], hold_f[...]) + nt(u_b[...], hold_b[...])
    two_copies = []
    for k, peer in enumerate(ahead):
        two_out[k] = terms[:, lanes(k, width)].astype(BF16)
        two_copies.append(send(two_out.at[k], two_in.at[k], node_sem, (3, k), {"node": peer}))

    for t in range(steps):
        base0[step(t), :] = nn(mix_t[lanes(0, chans)], rc_ref[step(t), :])
        mix0[step(t), :] = nn(mix_w[0], hid[step(t), :])
    last = step(steps - 1)
    base0[last, :] += nn(ws_ref[...], cs_ref[...])

    skip = nn(skip_w, hid[last, :])
    half = 128
    for g in range(skip.shape[0] // half):
        part = jnp.broadcast_to(bs_ref[:, lanes(g, half)], (half, half)).T
        part = jnp.concatenate([part] * (blocks * width // half), axis=1)
        skip_ref[lanes(g, half), :] = (skip[lanes(g, half), :] + part).astype(BF16)
    ones = jnp.ones((16, blocks * width), BF16)
    early[...] = jnp.zeros_like(early)
    late[...] = jnp.zeros_like(late)

    def put(buffer, top, value):
        rows = buffer.shape[1]
        value = value.astype(BF16)
        at = top
        while at < top + value.shape[0]:
            c, o = at // rows, at % rows
            n = min(rows - o, top + value.shape[0] - at)
            buffer[c, o : o + n, 0 : value.shape[1]] = value[at - top : at - top + n]
            at += n

    groups = [None] * 5
    mix_bias = None

    def plus(a, b):
        return b if a is None else a + b

    for t in range(steps):
        cot = rc_ref[step(t), :]
        groups[0] = plus(groups[0], nt(cot, hid[step(t), :]))
        groups[1] = plus(groups[1], nt(cot, hop_f[step(t), :]))
        groups[2] = plus(groups[2], nt(r1_f[step(t)], hop_f[step(t), :]))
        groups[3] = plus(groups[3], nt(cot, hop_b[step(t), :]))
        groups[4] = plus(groups[4], nt(r1_b[step(t)], hop_b[step(t), :]))
        mix_bias = plus(mix_bias, nt(ones, cot))
    skip_grad = nt(hid[last, :], cs_ref[...])
    skip_bias = nt(ones, cs_ref[...])
    put(early, 0, jnp.concatenate([groups[0], groups[1]], axis=1))
    put(early, chans, jnp.concatenate([groups[2], groups[3]], axis=1))
    put(early, 2 * chans, groups[4])
    bias_top = 3 * chans
    put(early, bias_top, mix_bias)
    for g in range(skips // 128):
        put(early, bias_top + 16 * (g + 1), skip_bias[:, lanes(g, 128)])
    skip_top = bias_top + 16 * (1 + skips // 128)
    for g in range(skips // 128):
        put(early, skip_top + g * chans, skip_grad[:, lanes(g, 128)])

    def scatter(buffer, landing, base):
        return [
            send(buffer.at[peer], landing.at[k], red_sem, (base + k,), {"batch": peer})
            for k, peer in enumerate(mates)
        ]

    def across(buffer, landing, nodes, copies, base):
        total = buffer[row].astype(F32)
        for k, copy in enumerate(copies):
            copy.wait_recv()
            total += landing[k].astype(F32)
        nodes[me] = total.astype(BF16)
        return [
            send(nodes.at[me], nodes.at[me], red_sem, (base + k,), {"node": peer})
            for k, peer in enumerate(ahead)
        ]

    def arrived(copies, nodes, sem_base):
        for k, peer in enumerate(behind):
            pltpu.make_async_remote_copy(
                src_ref=nodes.at[peer], dst_ref=nodes.at[peer],
                send_sem=red_sem.at[0, sem_base + k], recv_sem=red_sem.at[1, sem_base + k],
                device_id={"node": peer}, device_id_type=MESH,
            ).wait_recv()

    def gather(nodes, result, base):
        total = nodes[0].astype(F32)
        for k in range(1, n_node):
            total += nodes[k].astype(F32)
        result[row] = total.astype(BF16)
        return [
            send(result.at[row], result.at[row], red_sem, (base + k,), {"batch": peer})
            for k, peer in enumerate(mates)
        ]

    def gathered(result, base):
        for k in range(n_batch - 1):
            peer = lax.rem(row + n_batch - k - 1, n_batch)
            pltpu.make_async_remote_copy(
                src_ref=result.at[peer], dst_ref=result.at[peer],
                send_sem=red_sem.at[0, base + k], recv_sem=red_sem.at[1, base + k],
                device_id={"batch": peer}, device_id_type=MESH,
            ).wait_recv()

    span = 2 * (n_batch - 1) + n_node - 1
    at1, at2 = n_batch - 1, n_batch - 1 + n_node - 1
    early_copies = scatter(early, early_rs, 0)

    near_one = base0[...] + nn(one_f[...], dense_f[...]) + nn(one_b[...], dense_b[...])
    near_u = mix0[...] + nt(u_f[...], dense_f[...]) + nt(u_b[...], dense_b[...])

    for copy in back_copies:
        copy.wait_recv()
    conv_grad = None
    conv_bias = None
    placed = []
    for j in range(blocks):
        total = near_one[:, lanes(j, width)]
        for k in range(n_node - 1):
            total += back_in[k].astype(F32) * pick_mask(src_rows[k], j)
        placed.append(total)
    grad_hidden = jnp.concatenate(placed, axis=1).astype(BF16).astype(F32)
    for t in range(steps):
        f, s, g = filt[step(t), :], gate[step(t), :], grad_hidden[step(t)]
        gs = g * s
        both = jnp.concatenate([gs * (1.0 - f * f), gs * f * (1.0 - s)], axis=0).astype(BF16)
        pre[t] = both
        conv_grad = plus(conv_grad, nt(both, taps[t]))
        conv_bias = plus(conv_bias, nt(ones, both))
    put(late, 0, conv_grad)
    put(late, 2 * chans, conv_bias)
    late_copies = scatter(late, late_rs, span)
    early_node_copies = across(early, early_rs, early_node, early_copies, at1)

    for t in range(steps + DILATION_GAP):
        total = None
        if t < steps:
            total = nn(conv_t[:chans], pre[t])
        if t >= DILATION_GAP:
            total = plus(total, nn(conv_t[chans:], pre[t - DILATION_GAP]))
            total += rc_ref[step(t - DILATION_GAP), :].astype(F32)
        gx_ref[step(t), :] = total.astype(BF16)

    late_node_copies = across(late, late_rs, late_node, late_copies, span + at1)

    arrived(early_node_copies, early_node, at1)
    gather(early_node, early_all, at2)

    for copy in two_copies:
        copy.wait_recv()
    mix_col = jnp.broadcast_to(
        jnp.concatenate([bm_ref[...]] * (128 // chans), axis=1), (128, 128)
    ).T
    mix_col = jnp.concatenate([mix_col[:chans]] * steps, axis=0)
    for i in range(blocks):
        total = near_u[:, lanes(i, width)] + mix_col
        for k in range(n_node - 1):
            total += two_in[k].astype(F32) * dst_masks[k][i]
        total += x_ref[DILATION_GAP * chans :, lanes(i, width)].astype(F32)
        res_ref[:, lanes(i, width)] = total.astype(BF16)

    arrived(late_node_copies, late_node, span + at1)
    gather(late_node, late_all, span + at2)

    gathered(early_all, at2)
    early_ref[...] = early_all[...]
    gathered(late_all, span + at2)
    late_ref[...] = late_all[...]

    for copy in started:
        copy.wait_send()


def finish(
    sizes, res_in, skip_in, gx_in, early, late,
    res_ref, skip_ref, gx_ref, gwc_ref, gbc_ref, gwm_ref, gbm_ref, gws_ref, gbs_ref,
):
    chans, skips, scale = sizes
    res_ref[...] = res_in[...]
    skip_ref[...] = skip_in[...]
    gx_ref[...] = gx_in[...]

    def take(buffer, top, count):
        rows = buffer.shape[1]
        parts = []
        at = top
        while at < top + count:
            c, o = at // rows, at % rows
            n = min(rows - o, top + count - at)
            parts.append(buffer[c, o : o + n, :].astype(F32))
            at += n
        return (parts[0] if len(parts) == 1 else jnp.concatenate(parts, axis=0)) * scale

    gwm_ref[:, : 2 * chans] = take(early, 0, chans)
    gwm_ref[:, 2 * chans : 4 * chans] = take(early, chans, chans)
    gwm_ref[:, 4 * chans :] = take(early, 2 * chans, chans)[:, :chans]
    bias_top = 3 * chans
    gbm_ref[...] = take(early, bias_top, 16)[0:1, :chans]
    skip_top = bias_top + 16 * (1 + skips // 128)
    for g in range(skips // 128):
        gbs_ref[:, lanes(g, 128)] = take(early, bias_top + 16 * (g + 1), 16)[0:1]
        gws_ref[:, lanes(g, 128)] = take(early, skip_top + g * chans, chans)
    gwc_ref[...] = take(late, 0, 2 * chans)
    gbc_ref[...] = take(late, 2 * chans, 16)[0:1]


def shards(
    inputs, w_conv, b_conv, w_mix, b_mix, w_skip, b_skip, local_fwd, local_bwd,
    remote_fwd, remote_bwd, tile_src, tile_dst, residual_cotangent, cot_skip,
):
    n_node, n_batch = lax.axis_size("node"), lax.axis_size("batch")
    windows, input_steps, chans, local_nodes = inputs.shape
    steps = input_steps - DILATION_GAP
    width = remote_fwd.shape[1]
    skips = w_skip.shape[0]
    rows = steps * chans
    scale = 1.0 / math.sqrt(float(windows * n_batch * local_nodes * n_node * steps))
    peers = n_node - 1

    def chunk(total):
        return -(-total // (16 * n_batch)) * 16

    early = chunk(3 * chans + 16 * (1 + skips // 128) + skips // 128 * chans)
    late = chunk(2 * chans + 16)

    def field(kind):
        return pltpu.VMEM((rows, local_nodes), kind)

    def slots(*shape):
        return pltpu.VMEM((peers, *shape), BF16)

    scratch = (
        [pltpu.VMEM((local_nodes, local_nodes), BF16)] * 2
        + [pltpu.VMEM((peers * width, local_nodes), BF16)] * 2
        + [pltpu.VMEM((local_nodes, peers * width), BF16)] * 2
        + [pltpu.VMEM((peers, 8, 128), jnp.int32)] * 2
        + [pltpu.VMEM((2, peers, width, width), BF16)]
        + [slots(rows, width)] * 8
        + [field(F32), field(F32), field(BF16)]
        + [pltpu.VMEM((steps, 2 * chans, local_nodes), BF16)]
        + [field(F32)] * 8
        + [field(BF16)] * 6
    )
    for size in (early, late):
        scratch += [
            pltpu.VMEM((n_batch, size, 128), BF16),
            pltpu.VMEM((n_batch - 1, size, 128), BF16),
            pltpu.VMEM((n_node, size, 128), BF16),
            pltpu.VMEM((n_batch, size, 128), BF16),
        ]
    scratch += [
        pltpu.SemaphoreType.DMA((2, 2, peers)),
        pltpu.SemaphoreType.DMA((2, 5, peers)),
        pltpu.SemaphoreType.DMA((2, 2 * (2 * (n_batch - 1) + peers))),
    ]
    vmem = pl.BlockSpec(memory_space=pltpu.VMEM)
    smem = pl.BlockSpec(memory_space=pltpu.SMEM)
    results = pl.pallas_call(
        functools.partial(kernel, (n_node, n_batch, steps, chans, scale)),
        out_shape=[
            jax.ShapeDtypeStruct((rows, local_nodes), BF16),
            jax.ShapeDtypeStruct((skips, local_nodes), BF16),
            jax.ShapeDtypeStruct((input_steps * chans, local_nodes), BF16),
            jax.ShapeDtypeStruct((n_batch, early, 128), BF16),
            jax.ShapeDtypeStruct((n_batch, late, 128), BF16),
        ],
        in_specs=[vmem] * 11 + [smem] * 2 + [vmem] * 2,
        out_specs=[vmem] * 5,
        scratch_shapes=scratch,
        compiler_params=pltpu.CompilerParams(
            collective_id=0, has_side_effects=True, vmem_limit_bytes=56 * 1024 * 1024
        ),
        cost_estimate=pl.CostEstimate(
            flops=2_000_000_000, bytes_accessed=4_000_000, transcendentals=300_000
        ),
    )(
        inputs.reshape(input_steps * chans, local_nodes),
        w_conv, b_conv[None], w_mix, b_mix[None], w_skip.T, b_skip[None],
        local_fwd, local_bwd, remote_fwd, remote_bwd, tile_src, tile_dst,
        residual_cotangent.reshape(rows, local_nodes),
        cot_skip.reshape(skips, local_nodes),
    )
    res, skip, gx, gwc, gbc, gwm, gbm, gws, gbs = pl.pallas_call(
        functools.partial(finish, (chans, skips, scale)),
        out_shape=[
            *[jax.ShapeDtypeStruct(a.shape, a.dtype) for a in results[:3]],
            jax.ShapeDtypeStruct((2 * chans, 2 * chans), F32),
            jax.ShapeDtypeStruct((1, 2 * chans), F32),
            jax.ShapeDtypeStruct((chans, 5 * chans), F32),
            jax.ShapeDtypeStruct((1, chans), F32),
            jax.ShapeDtypeStruct((chans, skips), F32),
            jax.ShapeDtypeStruct((1, skips), F32),
        ],
        in_specs=[vmem] * 5,
        out_specs=[vmem] * 9,
        compiler_params=pltpu.CompilerParams(vmem_limit_bytes=56 * 1024 * 1024),
    )(*results)
    return (
        res.reshape(windows, steps, chans, local_nodes),
        skip.reshape(windows, skips, local_nodes),
        gx.reshape(windows, input_steps, chans, local_nodes),
        gwc, gbc[0], gwm, gbm[0], gws.T, gbs[0],
    )


def solution(mesh):
    return jax.shard_map(
        shards,
        mesh=mesh,
        in_specs=(
            P("batch", None, None, "node"),
            P(), P(), P(), P(), P(), P(),
            P("node", None),
            P("node", None),
            P("node", None, None),
            P("node", None, None),
            P("node"),
            P("node"),
            P("batch", None, None, "node"),
            P("batch", None, "node"),
        ),
        out_specs=(
            P("batch", None, None, "node"),
            P("batch", None, "node"),
            P("batch", None, None, "node"),
            P(), P(), P(), P(), P(), P(),
        ),
        check_vma=False,
    )
```
